32 devices in a mesh: shard: 4 (over y, core), rep: 8 (over z, x).
Axes of the slice: x: 2, y: 2, z: 4, core: 2. Of those that a mesh axis runs over, the one named last changes fastest.
Arguments:
- tokens: bfloat16 [16384, 896], P(('shard', 'rep')), may hold values from -6 to 6
- out_grad: bfloat16 [16384, 896], P(('shard', 'rep')), may hold values from -6 to 6
- segments: int32 [32, 512], P(('shard', 'rep')), may hold values from 0 to 7, never falling along the last dimension, each value on 1 to 256 neighbouring positions
- w_query: float32 [896, 896], P('shard'), may hold values from -0.1875 to 0.1875
- w_key: float32 [896, 128], P('shard'), may hold values from -0.1875 to 0.1875
- w_value: float32 [896, 128], P('shard'), may hold values from -0.1875 to 0.1875
- w_out: float32 [896, 896], P('shard'), may hold values from -0.75 to 0.75
- w_gate: float32 [896, 4864], P('shard'), may hold values from -0.1875 to 0.1875
- w_up: float32 [896, 4864], P('shard'), may hold values from -0.1875 to 0.1875
- w_down: float32 [4864, 896], P('shard'), may hold values from -0.078125 to 0.078125
- gains: float32 [2, 896], P(None, 'shard'), may hold values from 0.5 to 1.5
- biases: float32 [1152], P('shard'), may hold values from -3 to 3
- mom_query: float32 [896, 896], P('shard'), may hold values from -768 to 768
- mom_key: float32 [896, 128], P('shard'), may hold values from -768 to 768
- mom_value: float32 [896, 128], P('shard'), may hold values from -768 to 768
- mom_out: float32 [896, 896], P('shard'), may hold values from -160 to 160
- mom_gate: float32 [896, 4864], P('shard'), may hold values from -192 to 192
- mom_up: float32 [896, 4864], P('shard'), may hold values from -192 to 192
- mom_down: float32 [4864, 896], P('shard'), may hold values from -384 to 384
- gain_mom: float32 [2, 896], P(None, 'shard'), may hold values from -768 to 768
- bias_mom: float32 [1152], P('shard'), may hold values from -768 to 768
Outputs:
- result: bfloat16 [16384, 896], P(('shard', 'rep'))
- input_grad: float32 [16384, 896], P(('shard', 'rep'))
- mom_query_new: float32 [896, 896], P('shard')
- mom_key_new: float32 [896, 128], P('shard')
- mom_value_new: float32 [896, 128], P('shard')
- mom_out_new: float32 [896, 896], P('shard')
- mom_gate_new: float32 [896, 4864], P('shard')
- mom_up_new: float32 [896, 4864], P('shard')
- mom_down_new: float32 [4864, 896], P('shard')
- weight_query_new: float32 [896, 896], P('shard')
- weight_key_new: float32 [896, 128], P('shard')
- weight_value_new: float32 [896, 128], P('shard')
- weight_out_new: float32 [896, 896], P('shard')
- weight_gate_new: float32 [896, 4864], P('shard')
- weight_up_new: float32 [896, 4864], P('shard')
- weight_down_new: float32 [4864, 896], P('shard')
- gain_mom_new: float32 [2, 896], P(None, 'shard')
- gains_new: float32 [2, 896], P(None, 'shard')
- bias_mom_new: float32 [1152], P('shard')
- biases_new: float32 [1152], P('shard')
The draws below stay inside these ranges and needn't reach their ends.
Inputs may be any that keep to these rules, and one draw needn't show every extreme that they name: `segments`: segment numbers never fall along a row; a document holds at most 256 tokens.
All inputs are finite; a program needn't handle non-finite values.
Results may differ from the reference program's by a relative error of at most 0.012.
The reference program's roundings to bfloat16 on the way count: a program that leaves them out, or rounds other values in their place, can miss the bound.
Values may be sent and summed in bfloat16 or wider, within the bound.
A program may use at most 448 MiB of HBM per device.

```python
import math
import jax
import jax.numpy as jnp
import numpy as np
from jax import lax

D = 896
FF = 4864
QH = 14
KVH = 2
HD = 64
SEQ_LEN = 512
NS_ITERS = 5
SEQS = 32
TOKENS = 16384


def levels(stream_key, extent, shards, least, top_value):
    factor_of, own = 1.0, jax.random.fold_in(stream_key, 6)
    for axis_at, parts in shards:
        heights = jnp.exp(jax.random.uniform(jax.random.fold_in(own, axis_at), (parts,), jnp.float32, least / len(shards), top_value / len(shards)))
        factor_of = factor_of * jnp.repeat(heights, extent[axis_at] // parts).reshape([-1 if axis == axis_at else 1 for axis in range(len(extent))])
    return factor_of


def length_profile(number_of, total, reach, slope):
    loads = [(1 << 20) // math.isqrt(rank ** slope) + 1 for rank in range(2, number_of + 1)]
    surplus, counts = total - reach - (number_of - 1), [1] * (number_of - 1)
    while surplus > 0:
        free = [i for i in range(number_of - 1) if counts[i] < reach]
        pool, budget = sum([loads[i] for i in free]), surplus
        for i in free:
            more = min(reach - counts[i], max(1, budget * loads[i] // pool), surplus)
            counts[i] = counts[i] + more
            surplus = surplus - more
    return np.array([reach] + counts)


def uneven(key, count, total, bound, slope):
    if count == 2:
        one = jax.random.randint(key, (), max(1, total - bound), min(bound, total - 1) + 1)
        return jnp.stack([one, total - one])
    tallies = jnp.asarray(length_profile(count, total, bound, slope), jnp.int32)
    couples = (count - 1) // 2
    giver, receiver = tallies[1:1 + 2 * couples:2], tallies[2:2 + 2 * couples:2]
    room = jnp.minimum(giver - 1, bound - receiver)
    moved = jax.random.randint(jax.random.fold_in(key, 1), (couples,), 0, 1 << 20) % (room + 1)
    tallies = tallies.at[1:1 + 2 * couples:2].set(giver - moved).at[2:2 + 2 * couples:2].set(receiver + moved)
    return tallies[jax.random.permutation(jax.random.fold_in(key, 2), count)]


def bell_draw(rng, extent, deviation, limit, split=(), kind=jnp.bfloat16):
    entries = jax.random.normal(rng, extent, jnp.float32) * deviation
    if len(split) > 0:
        entries = levels(rng, extent, split, -0.22, 0.18) * entries
    return jnp.clip(entries, min=-limit, max=limit).astype(kind)


def setup_inputs(seed: int = 0) -> dict:
    arg_keys = jax.random.split(jax.random.key(seed), 22)
    return {
        "tokens": bell_draw(arg_keys[0], (TOKENS, D), 1.0, 6.0, ((0, 32),)),
        "out_grad": bell_draw(arg_keys[1], (TOKENS, D), 1.0, 6.0, ((0, 32),)),
        "segments": jax.vmap(lambda own: jnp.searchsorted(jnp.cumsum(uneven(own, 8, SEQ_LEN, SEQ_LEN // 2, 2)), jnp.arange(SEQ_LEN), side="right"))(jax.random.split(arg_keys[2], SEQS)).reshape((SEQS, SEQ_LEN)).astype(jnp.int32),
        "w_query": bell_draw(arg_keys[3], (D, D), D ** -0.5, 0.1875, ((0, 4),), jnp.float32),
        "w_key": bell_draw(arg_keys[4], (D, KVH * HD), D ** -0.5, 0.1875, ((0, 4),), jnp.float32),
        "w_value": bell_draw(arg_keys[5], (D, KVH * HD), D ** -0.5, 0.1875, ((0, 4),), jnp.float32),
        "w_out": bell_draw(arg_keys[6], (D, D), (D // 16) ** -0.5, 0.75, ((0, 4),), jnp.float32),
        "w_gate": bell_draw(arg_keys[7], (D, FF), D ** -0.5, 0.1875, ((0, 4),), jnp.float32),
        "w_up": bell_draw(arg_keys[8], (D, FF), D ** -0.5, 0.1875, ((0, 4),), jnp.float32),
        "w_down": bell_draw(arg_keys[9], (FF, D), FF ** -0.5, 0.078125, ((0, 4),), jnp.float32),
        "gains": jnp.clip(1.0 + 0.1 * jax.random.normal(arg_keys[10], (2, D), jnp.float32), 0.5, 1.5),
        "biases": bell_draw(arg_keys[11], (D + 2 * KVH * HD,), 0.5, 3.0, ((0, 4),), jnp.float32),
        "mom_query": bell_draw(arg_keys[12], (D, D), (TOKENS ** 0.5), 768.0, ((0, 4),), jnp.float32),
        "mom_key": bell_draw(arg_keys[13], (D, KVH * HD), (TOKENS ** 0.5), 768.0, ((0, 4),), jnp.float32),
        "mom_value": bell_draw(arg_keys[14], (D, KVH * HD), (TOKENS ** 0.5), 768.0, ((0, 4),), jnp.float32),
        "mom_out": bell_draw(arg_keys[15], (D, D), (0.2 * TOKENS ** 0.5), 160.0, ((0, 4),), jnp.float32),
        "mom_gate": bell_draw(arg_keys[16], (D, FF), (0.25 * TOKENS ** 0.5), 192.0, ((0, 4),), jnp.float32),
        "mom_up": bell_draw(arg_keys[17], (D, FF), (0.25 * TOKENS ** 0.5), 192.0, ((0, 4),), jnp.float32),
        "mom_down": bell_draw(arg_keys[18], (FF, D), (0.5 * TOKENS ** 0.5), 384.0, ((0, 4),), jnp.float32),
        "gain_mom": bell_draw(arg_keys[19], (2, D), (TOKENS ** 0.5), 768.0, ((1, 4),), jnp.float32),
        "bias_mom": bell_draw(arg_keys[20], (D + 2 * KVH * HD,), (TOKENS ** 0.5), 768.0, ((0, 4),), jnp.float32),
    }


@jax.custom_vjp
def low(v):
    return lax.optimization_barrier(v.astype(jnp.bfloat16)).astype(jnp.float32)

@jax.custom_vjp
def low_back(v):
    return v

def low_keep(v):
    return (low(v), None)

def low_pass(kept, grad):
    return (grad,)

def back_keep(v):
    return (v, None)

def back_low(kept, grad):
    return (low(grad),)
low.defvjp(low_keep, low_pass)
low_back.defvjp(back_keep, back_low)
eps_norm = 1e-06
theta_base = 1000000.0
coef_a = 3.4445
coef_b = -4.775
coef_c = 2.0315
momentum_decay = 0.9
muon_rate = 1.0
vector_rate = 0.1
masked_score = -1000000000.0
highest = lax.Precision.HIGHEST

def matmul(left, right):
    return jnp.dot(left, right, precision=highest)

def rope_tables(segments, head):
    length = segments.shape[-1]
    indices = jnp.arange(length, dtype=jnp.int32)
    first = jnp.ones(segments.shape[:-1] + (1,), dtype=jnp.bool_)
    change = jnp.concatenate([first, segments[..., 1:] != segments[..., :-1]], axis=-1)
    starts = lax.cummax(jnp.where(change, indices, 0), axis=segments.ndim - 1)
    place = (indices - starts).astype(jnp.float32)
    half_dim = head // 2
    inverse = jnp.exp(jnp.arange(half_dim, dtype=jnp.float32) * (-2.0 * math.log(theta_base) / head))
    angles = place[..., None] * inverse
    angles = jnp.concatenate([angles, angles], axis=-1)
    return (jnp.cos(angles), jnp.sin(angles))

def rotary(values, cosine, sine):
    half_dim = values.shape[-1] // 2
    turned = jnp.concatenate([-values[..., half_dim:], values[..., :half_dim]], axis=-1)
    return values * cosine + turned * sine

def norm_rows(values, gain):
    factor = lax.rsqrt(lax.optimization_barrier(jnp.mean(values * values, axis=-1, keepdims=True)) + eps_norm)
    return low(values * factor * gain)

def attend(item):
    queries, keys, values, seg_row = item
    length = seg_row.shape[0]
    grouped = queries.reshape(length, KVH, QH // KVH, HD)
    raw = jnp.einsum('qhgd,khd->hgqk', grouped, keys, precision=highest)
    scores = low_back(raw) * (1.0 / math.sqrt(HD))
    places = jnp.arange(length)
    allowed = (places[:, None] >= places[None, :]) & (seg_row[:, None] == seg_row[None, :])
    probs = low(jax.nn.softmax(jnp.where(allowed, scores, masked_score), axis=-1))
    joined = jnp.einsum('hgqk,khd->qhgd', probs, values, precision=highest)
    return joined.reshape(length, QH * HD)

def forward(params, inputs, seg_block):
    wq, wk, wv, wo, wg, wu, wd, gain_pair, bias_all = [low(item) for item in params]
    count, length, width = inputs.shape
    kv_width = KVH * HD
    flat = inputs.reshape(count * length, width)
    normed_one = norm_rows(flat, gain_pair[0])
    q_lin = low_back(matmul(normed_one, wq) + bias_all[:width])
    k_lin = low_back(matmul(normed_one, wk) + bias_all[width:width + kv_width])
    v_lin = low_back(matmul(normed_one, wv) + bias_all[width + kv_width:])
    cosine, sine = rope_tables(seg_block, HD)
    cosine = cosine[:, :, None, :]
    sine = sine[:, :, None, :]
    queries = low(rotary(q_lin.reshape(count, length, QH, HD), cosine, sine))
    keys = low(rotary(k_lin.reshape(count, length, KVH, HD), cosine, sine))
    values = low(v_lin).reshape(count, length, KVH, HD)
    attended = lax.map(jax.checkpoint(attend), (queries, keys, values, seg_block))
    attended = low(low_back(attended.reshape(count * length, width)))
    middle = flat + low_back(matmul(attended, wo))
    normed_two = norm_rows(middle, gain_pair[1])
    gate = low_back(matmul(normed_two, wg))
    upper = low_back(matmul(normed_two, wu))
    hidden = low(jax.nn.silu(gate) * upper)
    result = middle + low_back(matmul(hidden, wd))
    return result.reshape(count, length, width)

def orthogonal_part(matrix):
    tall = matrix.shape[0] > matrix.shape[1]
    work = matrix.T if tall else matrix
    work = work / (jnp.sqrt(jnp.sum(work * work)) + 1e-07)
    for turn in range(NS_ITERS):
        square = jnp.dot(work, work.T, precision=highest)
        mixed = coef_b * square + coef_c * jnp.dot(square, square, precision=highest)
        work = coef_a * work + jnp.dot(mixed, work, precision=highest)
    return work.T if tall else work

def reference(tokens, out_grad, segments, w_query, w_key, w_value, w_out, w_gate, w_up, w_down, gains, biases, mom_query, mom_key, mom_value, mom_out, mom_gate, mom_up, mom_down, gain_mom, bias_mom):
    params = (w_query, w_key, w_value, w_out, w_gate, w_up, w_down, gains, biases)
    seq_count = segments.shape[0]
    per_step = math.gcd(seq_count, max(1, 4096 // SEQ_LEN))
    step_count = seq_count // per_step
    inputs = tokens.astype(jnp.float32).reshape(step_count, per_step, SEQ_LEN, D)
    cotangent = out_grad.astype(jnp.float32).reshape(step_count, per_step, SEQ_LEN, D)
    seg_steps = segments.reshape(step_count, per_step, SEQ_LEN)

    def one_step(totals, item):
        block_in, block_grad, block_seg = item

        def run(weights, values):
            return forward(weights, values, block_seg)
        block_out, pullback = jax.vjp(run, params, block_in)
        grad_params, grad_in = pullback(block_grad)
        totals = jax.tree.map(lambda left, right: left + right, totals, grad_params)
        return (totals, (block_out, grad_in))
    zeros = jax.tree.map(jnp.zeros_like, params)
    totals, (outputs, input_grads) = lax.scan(one_step, zeros, (inputs, cotangent, seg_steps))
    result = outputs.reshape(TOKENS, D).astype(jnp.bfloat16)
    input_grad = input_grads.reshape(TOKENS, D)
    masters = (w_query, w_key, w_value, w_out, w_gate, w_up, w_down)
    moments = (mom_query, mom_key, mom_value, mom_out, mom_gate, mom_up, mom_down)
    new_moms = []
    new_weights = []
    for index in range(7):
        fresh = momentum_decay * moments[index] + totals[index]
        rows, cols = masters[index].shape
        factor = muon_rate * math.sqrt(max(rows, cols) / rows)
        new_moms.append(fresh)
        new_weights.append(masters[index] - factor * orthogonal_part(fresh))
    gain_mom_new = momentum_decay * gain_mom + totals[7]
    gains_new = gains - vector_rate * gain_mom_new / math.sqrt(TOKENS)
    bias_mom_new = momentum_decay * bias_mom + totals[8]
    biases_new = biases - vector_rate * bias_mom_new / math.sqrt(TOKENS)
    return (result, input_grad, new_moms[0], new_moms[1], new_moms[2], new_moms[3], new_moms[4], new_moms[5], new_moms[6], new_weights[0], new_weights[1], new_weights[2], new_weights[3], new_weights[4], new_weights[5], new_weights[6], gain_mom_new, gains_new, bias_mom_new, biases_new)
```

```python
import math

import jax
import jax.numpy as jnp
from jax import lax
from jax.sharding import PartitionSpec as P

D = 896
QH = 14
KVH = 2
HD = 64
NS_ITERS = 5


eps_norm = 1e-06
theta_base = 1000000.0
coef_a = 3.4445
coef_b = -4.775
coef_c = 2.0315
momentum_decay = 0.9
muon_rate = 1.0
vector_rate = 0.1
masked_score = -1000000000.0
highest = lax.Precision.HIGHEST


def for_sending(array):

    def short(part):
        return part.astype(jnp.bfloat16) if part.dtype == jnp.float32 else part

    return jax.tree.map(short, array)


def product(left, right):
    return jnp.dot(left, right, preferred_element_type=jnp.float32)


def left_product(left, right):
    return lax.dot_general(
        left, right, (((0,), (0,)), ((), ())), preferred_element_type=jnp.float32
    )


def right_product(left, right):
    return lax.dot_general(
        left, right, (((1,), (1,)), ((), ())), preferred_element_type=jnp.float32
    )


def rope_tables(segments, head):
    length = segments.shape[-1]
    indices = jnp.arange(length, dtype=jnp.int32)
    first = jnp.ones(segments.shape[:-1] + (1,), dtype=jnp.bool_)
    change = jnp.concatenate([first, segments[..., 1:] != segments[..., :-1]], axis=-1)
    starts = lax.cummax(jnp.where(change, indices, 0), axis=segments.ndim - 1)
    place = (indices - starts).astype(jnp.float32)
    half_dim = head // 2
    inverse = jnp.exp(
        jnp.arange(half_dim, dtype=jnp.float32) * (-2.0 * math.log(theta_base) / head)
    )
    angles = place[..., None] * inverse
    angles = jnp.concatenate([angles, angles], axis=-1)
    return (jnp.cos(angles), jnp.sin(angles))


def rotary(values, cosine, sine):
    half_dim = values.shape[-1] // 2
    turned = jnp.concatenate([-values[..., half_dim:], values[..., :half_dim]], axis=-1)
    return values * cosine + turned * sine


def unrotary(grads, cosine, sine):
    half_dim = grads.shape[-1] // 2
    scaled = grads * sine
    turned = jnp.concatenate([scaled[..., half_dim:], -scaled[..., :half_dim]], axis=-1)
    return grads * cosine + turned


def norm_rows(values, gain):
    factor = lax.rsqrt(jnp.mean(values * values, axis=-1, keepdims=True) + eps_norm)
    unit = values * factor
    return (unit, factor, (unit * gain).astype(jnp.bfloat16))


def norm_back(grad_out, unit, factor, gain):
    grad_unit = grad_out * gain
    grad_gain = jnp.sum(grad_out * unit, axis=0)
    grad_in = factor * (grad_unit - unit * jnp.mean(grad_unit * unit, axis=-1, keepdims=True))
    return (grad_in, grad_gain)


def near(left, right):
    return jnp.dot(left, right, precision=lax.Precision.HIGH)


def gram_of_columns(rows):
    return lax.dot_general(
        rows, rows, (((0,), (0,)), ((), ())), precision=lax.Precision.HIGH
    )


def orthogonal_factor(gram):
    size = gram.shape[-1]
    norm = jnp.sqrt(jnp.trace(gram)) + 1e-07
    scale = 1.0 / norm
    square = gram * scale * scale
    eye = jnp.eye(size, dtype=jnp.float32)
    factor = None
    for turn in range(NS_ITERS):
        mixed = coef_b * square + coef_c * near(square, square)
        if factor is None:
            factor = coef_a * eye + mixed
        else:
            factor = coef_a * factor + near(factor, mixed)
        if turn < NS_ITERS - 1:
            half = coef_a * square + near(square, mixed)
            square = coef_a * half + near(half, mixed)
    return factor * scale


def pieces_of(rows, replicas):
    return 8 * math.ceil(rows / (8 * replicas))


def lengthened(block, rows):
    return jnp.pad(block, ((0, rows - block.shape[0]), (0, 0)))


def spread(values, group, size):
    count, width = values.shape
    parts = values.reshape(count, group, width // group)
    parts = jnp.pad(parts, ((0, 0), (0, 0), (0, size - width // group)))
    return parts.reshape(count, group * size)


def gathered_rows(array, group, rows):
    size = array.shape[0] // group
    return array.reshape(group, size, array.shape[1])[:, :rows].reshape(group * rows, array.shape[1])


def fetch(block, replica, size):
    piece = lax.dynamic_slice_in_dim(block, replica * size, size, axis=0)
    return lax.all_gather(piece, ("shard", "rep"), axis=0, tiled=True)


def total(grad):
    return lax.psum_scatter(
        grad.astype(jnp.bfloat16), ("shard", "rep"), scatter_dimension=0, tiled=True
    ).astype(jnp.float32)


def renew(momentum, grad, replica, size):
    piece = lax.dynamic_slice_in_dim(momentum, replica * size, size, axis=0)
    fresh = (momentum_decay * piece + total(grad)).astype(jnp.bfloat16)
    return lax.all_gather(fresh, ("shard", "rep"), axis=0, tiled=True)


def own_rows(array, place, group, rows):
    size = array.shape[0] // group
    return lax.dynamic_slice_in_dim(array, place * size, rows, axis=0).astype(jnp.float32)


def local(
    tokens,
    out_grad,
    segments,
    w_query,
    w_key,
    w_value,
    w_out,
    w_gate,
    w_up,
    w_down,
    gains,
    biases,
    mom_query,
    mom_key,
    mom_value,
    mom_out,
    mom_gate,
    mom_up,
    mom_down,
    gain_mom,
    bias_mom,
):
    group = lax.axis_size("shard")
    replicas = lax.axis_size("rep")
    kv_width = KVH * HD
    length = tokens.shape[0]
    place = lax.axis_index("shard")
    replica = lax.axis_index("rep")
    rows = w_gate.shape[0]
    down_rows = w_down.shape[0]
    size = pieces_of(rows, replicas)
    down_size = pieces_of(down_rows, replicas)
    tall = size * replicas
    down_tall = down_size * replicas
    attn_width = 2 * D + 2 * kv_width

    def vectors(pair, line):
        row = jnp.concatenate([pair[0], pair[1], line])
        return jnp.pad(row, (0, attn_width - row.shape[0]))[None]

    def attn_block(query, key, value, out, pair, line):
        block = jnp.concatenate([query, key, value, out], axis=1)
        return lengthened(jnp.concatenate([block, vectors(pair, line)], axis=0), tall)

    low_attn = attn_block(w_query, w_key, w_value, w_out, gains, biases).astype(jnp.bfloat16)
    low_gate = lengthened(w_gate.astype(jnp.bfloat16), tall)
    low_up = lengthened(w_up.astype(jnp.bfloat16), tall)
    low_down = lengthened(w_down.astype(jnp.bfloat16), down_tall)
    full_attn = fetch(low_attn, replica, size)
    full_gate = fetch(low_gate, replica, size)
    full_up = fetch(low_up, replica, size)
    full_down = gathered_rows(fetch(low_down, replica, down_size), group, down_rows)
    full_qkv = full_attn[:, : D + 2 * kv_width]
    full_out = full_attn[:, D + 2 * kv_width :]
    lines = full_attn.reshape(group, tall, attn_width)[:, rows]
    bias_rows = biases.shape[0]
    gain_one = lines[:, :rows].reshape(D).astype(jnp.float32)
    gain_two = lines[:, rows : 2 * rows].reshape(D).astype(jnp.float32)
    bias_all = lines[:, 2 * rows : 2 * rows + bias_rows].reshape(group * bias_rows).astype(jnp.float32)
    inputs = tokens.astype(jnp.float32)
    unit_one, factor_one, normed_one = norm_rows(inputs, gain_one)
    normed_one = spread(normed_one, group, tall)
    lin = product(normed_one, full_qkv) + bias_all
    query_lin = lin[:, :D]
    key_lin = lin[:, D : D + kv_width]
    value_lin = lin[:, D + kv_width :]
    seg_row = segments[0]
    cosine, sine = rope_tables(seg_row, HD)
    cosine = cosine[:, None, :]
    sine = sine[:, None, :]
    queries = rotary(query_lin.reshape(length, QH, HD), cosine, sine).astype(jnp.bfloat16)
    keys = rotary(key_lin.reshape(length, KVH, HD), cosine, sine).astype(jnp.bfloat16)
    values = value_lin.astype(jnp.bfloat16).reshape(length, KVH, HD)
    grouped = queries.reshape(length, KVH, QH // KVH, HD)
    score_scale = 1.0 / math.sqrt(HD)
    places = jnp.arange(length)
    allowed = (places[:, None] >= places[None, :]) & (seg_row[:, None] == seg_row[None, :])
    scores = (
        jnp.einsum("qhgd,khd->hgqk", grouped, keys, preferred_element_type=jnp.float32)
        * score_scale
    )
    probs = jax.nn.softmax(jnp.where(allowed, scores, masked_score), axis=-1)
    probs_low = probs.astype(jnp.bfloat16)
    attended = jnp.einsum("hgqk,khd->qhgd", probs_low, values, preferred_element_type=jnp.float32)
    attended = attended.reshape(length, D).astype(jnp.bfloat16)
    attended = spread(attended, group, tall)
    middle = inputs + product(attended, full_out)
    unit_two, factor_two, normed_two = norm_rows(middle, gain_two)
    normed_two = spread(normed_two, group, tall)
    gate_val = product(normed_two, full_gate)
    up_val = product(normed_two, full_up)
    sigma = jax.nn.sigmoid(gate_val)
    swish = gate_val * sigma
    hidden = (swish * up_val).astype(jnp.bfloat16)
    result = (middle + product(hidden, full_down)).astype(jnp.bfloat16)

    def narrowed(values):
        return values.reshape(length, group, tall)[:, :, :rows].reshape(length, D)

    cotangent = out_grad.astype(jnp.float32)
    grad_down = left_product(hidden, out_grad)
    dhidden = right_product(out_grad, full_down)
    dgate = (dhidden * up_val * sigma * (1.0 + gate_val * (1.0 - sigma))).astype(jnp.bfloat16)
    dup = (dhidden * swish).astype(jnp.bfloat16)
    grad_gate = left_product(normed_two, dgate)
    grad_up = left_product(normed_two, dup)
    dnormed_two = right_product(dgate, full_gate) + right_product(dup, full_up)
    dnormed_two = narrowed(dnormed_two)
    dmiddle_norm, grad_gain_two = norm_back(dnormed_two, unit_two, factor_two, gain_two)
    dmiddle = cotangent + dmiddle_norm
    dmid_low = dmiddle.astype(jnp.bfloat16)
    grad_out = left_product(attended, dmid_low)
    dattended = (
        narrowed(right_product(dmid_low, full_out)).astype(jnp.bfloat16).reshape(length, KVH, QH // KVH, HD)
    )
    dvalues = jnp.einsum("hgqk,qhgd->khd", probs_low, dattended, preferred_element_type=jnp.float32)
    dvalues = dvalues.reshape(length, kv_width).astype(jnp.bfloat16)
    dprobs = jnp.einsum("qhgd,khd->hgqk", dattended, values, preferred_element_type=jnp.float32)
    dscores = (
        probs * (dprobs - jnp.sum(probs * dprobs, axis=-1, keepdims=True)) * score_scale
    ).astype(jnp.bfloat16)
    dquery = jnp.einsum(
        "hgqk,khd->qhgd", dscores, keys, preferred_element_type=jnp.float32
    ).reshape(length, QH, HD)
    dkey = jnp.einsum("hgqk,qhgd->khd", dscores, grouped, preferred_element_type=jnp.float32)
    dquery = unrotary(dquery, cosine, sine).reshape(length, D).astype(jnp.bfloat16)
    dkey = unrotary(dkey, cosine, sine).reshape(length, kv_width).astype(jnp.bfloat16)
    dqkv = jnp.concatenate([dquery, dkey, dvalues], axis=1)
    grad_qkv = left_product(normed_one, dqkv)
    grad_biases = jnp.sum(dqkv.astype(jnp.float32), axis=0)
    dnormed_one = narrowed(right_product(dqkv, full_qkv))
    dinput_norm, grad_gain_one = norm_back(dnormed_one, unit_one, factor_one, gain_one)
    input_grad = dmiddle + dinput_norm
    grad_attn = jnp.concatenate([grad_qkv, grad_out], axis=1)
    grad_lines = jnp.concatenate(
        [
            grad_gain_one.reshape(group, rows),
            grad_gain_two.reshape(group, rows),
            grad_biases.reshape(group, bias_rows),
        ],
        axis=1,
    )
    grad_lines = jnp.pad(grad_lines, ((0, 0), (0, attn_width - 2 * rows - bias_rows)))
    grad_attn = grad_attn.reshape(group, tall, attn_width)
    grad_attn = jnp.concatenate(
        [grad_attn[:, :rows], grad_lines[:, None], grad_attn[:, rows + 1 :]], axis=1
    ).reshape(group * tall, attn_width)
    grad_down = jnp.pad(
        grad_down.astype(jnp.bfloat16).reshape(group, down_rows, D),
        ((0, 0), (0, down_tall - down_rows), (0, 0)),
    ).reshape(group * down_tall, D)
    mom_attn = attn_block(mom_query, mom_key, mom_value, mom_out, gain_mom, bias_mom)
    whole_down = renew(lengthened(mom_down, down_tall), grad_down, replica, down_size)
    whole_gate = renew(lengthened(mom_gate, tall), grad_gate, replica, size)
    whole_up = renew(lengthened(mom_up, tall), grad_up, replica, size)
    whole_attn = renew(mom_attn, grad_attn, replica, size)
    new_gate = own_rows(whole_gate, place, group, rows)
    new_up = own_rows(whole_up, place, group, rows)
    new_down = own_rows(whole_down, place, group, down_rows)
    new_attn = own_rows(whole_attn, place, group, rows)
    new_line = lax.dynamic_slice_in_dim(whole_attn, place * tall + rows, 1, axis=0)[0].astype(jnp.float32)
    new_query = new_attn[:, :D]
    new_key = new_attn[:, D : D + kv_width]
    new_value = new_attn[:, D + kv_width : D + 2 * kv_width]
    new_out = new_attn[:, D + 2 * kv_width :]
    token_total = length * group * replicas
    gain_mom_new = new_line[: 2 * rows].reshape(2, rows)
    gains_new = gains - vector_rate * gain_mom_new / math.sqrt(token_total)
    bias_mom_new = new_line[2 * rows : 2 * rows + bias_rows]
    biases_new = biases - vector_rate * bias_mom_new / math.sqrt(token_total)
    odd = replica % 2 == 1
    flat_attn = gathered_rows(whole_attn, group, rows)
    square_query = flat_attn[:, :D]
    square_out = flat_attn[:, D + 2 * kv_width :]

    def row_gram(whole):
        gram = right_product(whole, whole).reshape(group, tall, group, tall)
        return gram[:, :rows, :, :rows].reshape(D, D)

    def column_gram(whole):
        return left_product(whole, whole)

    gram = lax.switch(
        jnp.minimum(place, 3),
        [
            lambda: row_gram(whole_gate),
            lambda: row_gram(whole_up),
            lambda: column_gram(whole_down),
            lambda: column_gram(jnp.where(odd, square_out, square_query)),
        ],
    )
    factor = orthogonal_factor(gram).astype(jnp.bfloat16)
    factors = lax.all_gather(factor, "shard", axis=0, tiled=False)
    pairs = [(item, item ^ 1) for item in range(replicas)]
    other = lax.ppermute(factors[3], "rep", pairs)
    factor_query = jnp.where(odd, other, factors[3])
    factor_out = jnp.where(odd, factors[3], other)
    wide = math.sqrt(w_gate.shape[1] / D)

    def slab(item):
        block = lax.dynamic_slice_in_dim(factors[item], place * rows, rows, axis=0)
        return spread(block, group, tall)

    step_gate = wide * product(slab(0), whole_gate)
    step_up = wide * product(slab(1), whole_up)
    step_down = product(new_down.astype(jnp.bfloat16), factors[2])
    step_query = product(new_query.astype(jnp.bfloat16), factor_query)
    step_out = product(new_out.astype(jnp.bfloat16), factor_out)
    step_key = near(new_key, orthogonal_factor(column_gram(flat_attn[:, D : D + kv_width])))
    step_value = near(
        new_value, orthogonal_factor(column_gram(flat_attn[:, D + kv_width : D + 2 * kv_width]))
    )
    upd_gate = w_gate - muon_rate * step_gate
    upd_up = w_up - muon_rate * step_up
    upd_down = w_down - muon_rate * step_down
    upd_query = w_query - muon_rate * step_query
    upd_out = w_out - muon_rate * step_out
    upd_key = w_key - muon_rate * step_key
    upd_value = w_value - muon_rate * step_value
    return (
        result,
        input_grad,
        new_query,
        new_key,
        new_value,
        new_out,
        new_gate,
        new_up,
        new_down,
        upd_query,
        upd_key,
        upd_value,
        upd_out,
        upd_gate,
        upd_up,
        upd_down,
        gain_mom_new,
        gains_new,
        bias_mom_new,
        biases_new,
    )


def solution(mesh):
    placed = (
        P(("shard", "rep"), None),
        P(("shard", "rep"), None),
        P(("shard", "rep"), None),
        P("shard", None),
        P("shard", None),
        P("shard", None),
        P("shard", None),
        P("shard", None),
        P("shard", None),
        P("shard", None),
        P(None, "shard"),
        P("shard"),
        P("shard", None),
        P("shard", None),
        P("shard", None),
        P("shard", None),
        P("shard", None),
        P("shard", None),
        P("shard", None),
        P(None, "shard"),
        P("shard"),
    )
    return jax.shard_map(
        local,
        mesh=mesh,
        in_specs=placed,
        out_specs=(
            P(("shard", "rep"), None),
            P(("shard", "rep"), None),
            P("shard", None),
            P("shard", None),
            P("shard", None),
            P("shard", None),
            P("shard", None),
            P("shard", None),
            P("shard", None),
            P("shard", None),
            P("shard", None),
            P("shard", None),
            P("shard", None),
            P("shard", None),
            P("shard", None),
            P("shard", None),
            P(None, "shard"),
            P(None, "shard"),
            P("shard"),
            P("shard"),
        ),
        check_vma=False,
    )
```

```python
import math

import jax
import jax.numpy as jnp
from jax import lax
from jax.sharding import PartitionSpec as P

D = 896
QH = 14
KVH = 2
HD = 64
NS_ITERS = 5


eps_norm = 1e-06
theta_base = 1000000.0
coef_a = 3.4445
coef_b = -4.775
coef_c = 2.0315
momentum_decay = 0.9
muon_rate = 1.0
vector_rate = 0.1
masked_score = -1000000000.0
highest = lax.Precision.HIGHEST


def for_sending(array):

    def short(part):
        return part.astype(jnp.bfloat16) if part.dtype == jnp.float32 else part

    return jax.tree.map(short, array)


def product(left, right):
    return jnp.dot(left, right, preferred_element_type=jnp.float32)


def left_product(left, right):
    return lax.dot_general(
        left, right, (((0,), (0,)), ((), ())), preferred_element_type=jnp.float32
    )


def right_product(left, right):
    return lax.dot_general(
        left, right, (((1,), (1,)), ((), ())), preferred_element_type=jnp.float32
    )


def rope_tables(segments, head):
    length = segments.shape[-1]
    indices = jnp.arange(length, dtype=jnp.int32)
    first = jnp.ones(segments.shape[:-1] + (1,), dtype=jnp.bool_)
    change = jnp.concatenate([first, segments[..., 1:] != segments[..., :-1]], axis=-1)
    starts = lax.cummax(jnp.where(change, indices, 0), axis=segments.ndim - 1)
    place = (indices - starts).astype(jnp.float32)
    half_dim = head // 2
    inverse = jnp.exp(
        jnp.arange(half_dim, dtype=jnp.float32) * (-2.0 * math.log(theta_base) / head)
    )
    angles = place[..., None] * inverse
    angles = jnp.concatenate([angles, angles], axis=-1)
    return (jnp.cos(angles), jnp.sin(angles))


def rotary(values, cosine, sine):
    half_dim = values.shape[-1] // 2
    turned = jnp.concatenate([-values[..., half_dim:], values[..., :half_dim]], axis=-1)
    return values * cosine + turned * sine


def unrotary(grads, cosine, sine):
    half_dim = grads.shape[-1] // 2
    scaled = grads * sine
    turned = jnp.concatenate([scaled[..., half_dim:], -scaled[..., :half_dim]], axis=-1)
    return grads * cosine + turned


def norm_rows(values, gain):
    factor = lax.rsqrt(jnp.mean(values * values, axis=-1, keepdims=True) + eps_norm)
    unit = values * factor
    return (unit, factor, (unit * gain).astype(jnp.bfloat16))


def norm_back(grad_out, unit, factor, gain):
    grad_unit = grad_out * gain
    grad_gain = jnp.sum(grad_out * unit, axis=0)
    grad_in = factor * (grad_unit - unit * jnp.mean(grad_unit * unit, axis=-1, keepdims=True))
    return (grad_in, grad_gain)


def near(left, right):
    return jnp.dot(left, right, precision=lax.Precision.HIGH)


def gram_of_columns(rows):
    return lax.dot_general(
        rows, rows, (((0,), (0,)), ((), ())), precision=lax.Precision.HIGH
    )


def orthogonal_factor(gram):
    size = gram.shape[-1]
    norm = jnp.sqrt(jnp.trace(gram)) + 1e-07
    scale = 1.0 / norm
    square = gram * scale * scale
    eye = jnp.eye(size, dtype=jnp.float32)
    factor = None
    for turn in range(NS_ITERS):
        mixed = coef_b * square + coef_c * near(square, square)
        if factor is None:
            factor = coef_a * eye + mixed
        else:
            factor = coef_a * factor + near(factor, mixed)
        if turn < NS_ITERS - 1:
            half = coef_a * square + near(square, mixed)
            square = coef_a * half + near(half, mixed)
    return factor * scale


def pieces_of(rows, replicas):
    return 8 * math.ceil(rows / (8 * replicas))


def lengthened(block, rows):
    return jnp.pad(block, ((0, rows - block.shape[0]), (0, 0)))


def spread(values, group, size):
    count, width = values.shape
    parts = values.reshape(count, group, width // group)
    parts = jnp.pad(parts, ((0, 0), (0, 0), (0, size - width // group)))
    return parts.reshape(count, group * size)


def gathered_rows(array, group, rows):
    size = array.shape[0] // group
    return array.reshape(group, size, array.shape[1])[:, :rows].reshape(group * rows, array.shape[1])


def fetch(block):
    return lax.all_gather(block, "shard", axis=0, tiled=True)


def group_total(grad):
    return lax.psum_scatter(
        grad.astype(jnp.bfloat16), "shard", scatter_dimension=0, tiled=True
    )


def total(part, rows):
    return lax.psum_scatter(
        lengthened(part, rows), "rep", scatter_dimension=0, tiled=True
    )


def renew(momentum, summed, replica, size):
    piece = lax.dynamic_slice_in_dim(momentum, replica * size, size, axis=0)
    fresh = (momentum_decay * piece + summed.astype(jnp.float32)).astype(jnp.bfloat16)
    return lax.all_gather(fresh, ("shard", "rep"), axis=0, tiled=True)


def own_rows(array, place, group, rows):
    size = array.shape[0] // group
    return lax.dynamic_slice_in_dim(array, place * size, rows, axis=0).astype(jnp.float32)


def local(
    tokens,
    out_grad,
    segments,
    w_query,
    w_key,
    w_value,
    w_out,
    w_gate,
    w_up,
    w_down,
    gains,
    biases,
    mom_query,
    mom_key,
    mom_value,
    mom_out,
    mom_gate,
    mom_up,
    mom_down,
    gain_mom,
    bias_mom,
):
    group = lax.axis_size("shard")
    replicas = lax.axis_size("rep")
    kv_width = KVH * HD
    length = tokens.shape[0]
    place = lax.axis_index("shard")
    replica = lax.axis_index("rep")
    rows = w_gate.shape[0]
    down_rows = w_down.shape[0]
    size = pieces_of(rows, replicas)
    down_size = pieces_of(down_rows, replicas)
    tall = size * replicas
    down_tall = down_size * replicas
    attn_width = 2 * D + 2 * kv_width

    def vectors(pair, line):
        row = jnp.concatenate([pair[0], pair[1], line])
        return jnp.pad(row, (0, attn_width - row.shape[0]))[None]

    def attn_block(query, key, value, out, pair, line):
        block = jnp.concatenate([query, key, value, out], axis=1)
        return lengthened(jnp.concatenate([block, vectors(pair, line)], axis=0), tall)

    low_attn = attn_block(w_query, w_key, w_value, w_out, gains, biases).astype(jnp.bfloat16)
    full_attn = fetch(low_attn)
    full_gate = fetch(w_gate.astype(jnp.bfloat16))
    full_up = fetch(w_up.astype(jnp.bfloat16))
    full_down = fetch(w_down.astype(jnp.bfloat16))
    full_qkv = full_attn[:, : D + 2 * kv_width]
    full_out = full_attn[:, D + 2 * kv_width :]
    lines = full_attn.reshape(group, tall, attn_width)[:, rows]
    bias_rows = biases.shape[0]
    gain_one = lines[:, :rows].reshape(D).astype(jnp.float32)
    gain_two = lines[:, rows : 2 * rows].reshape(D).astype(jnp.float32)
    bias_all = lines[:, 2 * rows : 2 * rows + bias_rows].reshape(group * bias_rows).astype(jnp.float32)
    inputs = tokens.astype(jnp.float32)
    unit_one, factor_one, normed_one = norm_rows(inputs, gain_one)
    normed_one = spread(normed_one, group, tall)
    lin = product(normed_one, full_qkv) + bias_all
    query_lin = lin[:, :D]
    key_lin = lin[:, D : D + kv_width]
    value_lin = lin[:, D + kv_width :]
    seg_row = segments[0]
    cosine, sine = rope_tables(seg_row, HD)
    cosine = cosine[:, None, :]
    sine = sine[:, None, :]
    queries = rotary(query_lin.reshape(length, QH, HD), cosine, sine).astype(jnp.bfloat16)
    keys = rotary(key_lin.reshape(length, KVH, HD), cosine, sine).astype(jnp.bfloat16)
    values = value_lin.astype(jnp.bfloat16).reshape(length, KVH, HD)
    grouped = queries.reshape(length, KVH, QH // KVH, HD)
    score_scale = 1.0 / math.sqrt(HD)
    places = jnp.arange(length)
    allowed = (places[:, None] >= places[None, :]) & (seg_row[:, None] == seg_row[None, :])
    scores = (
        jnp.einsum("qhgd,khd->hgqk", grouped, keys, preferred_element_type=jnp.float32)
        * score_scale
    )
    probs = jax.nn.softmax(jnp.where(allowed, scores, masked_score), axis=-1)
    probs_low = probs.astype(jnp.bfloat16)
    attended = jnp.einsum("hgqk,khd->qhgd", probs_low, values, preferred_element_type=jnp.float32)
    attended = attended.reshape(length, D).astype(jnp.bfloat16)
    attended = spread(attended, group, tall)
    middle = inputs + product(attended, full_out)
    unit_two, factor_two, normed_two = norm_rows(middle, gain_two)
    gate_val = product(normed_two, full_gate)
    up_val = product(normed_two, full_up)
    sigma = jax.nn.sigmoid(gate_val)
    swish = gate_val * sigma
    hidden = (swish * up_val).astype(jnp.bfloat16)
    result = (middle + product(hidden, full_down)).astype(jnp.bfloat16)

    def narrowed(values):
        return values.reshape(length, group, tall)[:, :, :rows].reshape(length, D)

    cotangent = out_grad.astype(jnp.float32)
    grad_down = left_product(hidden, out_grad)
    dhidden = right_product(out_grad, full_down)
    dgate = (dhidden * up_val * sigma * (1.0 + gate_val * (1.0 - sigma))).astype(jnp.bfloat16)
    dup = (dhidden * swish).astype(jnp.bfloat16)
    grad_gate = left_product(normed_two, dgate)
    grad_up = left_product(normed_two, dup)
    dnormed_two = right_product(dgate, full_gate) + right_product(dup, full_up)
    grad_down, grad_gate, grad_up = for_sending((grad_down, grad_gate, grad_up))
    grad_down, grad_gate, grad_up, dnormed_two = lax.optimization_barrier(
        (grad_down, grad_gate, grad_up, dnormed_two)
    )
    dmiddle_norm, grad_gain_two = norm_back(dnormed_two, unit_two, factor_two, gain_two)
    dmiddle = cotangent + dmiddle_norm
    dmid_low = dmiddle.astype(jnp.bfloat16)
    grad_out = left_product(attended, dmid_low)
    dattended = (
        narrowed(right_product(dmid_low, full_out)).astype(jnp.bfloat16).reshape(length, KVH, QH // KVH, HD)
    )
    dvalues = jnp.einsum("hgqk,qhgd->khd", probs_low, dattended, preferred_element_type=jnp.float32)
    dvalues = dvalues.reshape(length, kv_width).astype(jnp.bfloat16)
    dprobs = jnp.einsum("qhgd,khd->hgqk", dattended, values, preferred_element_type=jnp.float32)
    dscores = (
        probs * (dprobs - jnp.sum(probs * dprobs, axis=-1, keepdims=True)) * score_scale
    ).astype(jnp.bfloat16)
    dquery = jnp.einsum(
        "hgqk,khd->qhgd", dscores, keys, preferred_element_type=jnp.float32
    ).reshape(length, QH, HD)
    dkey = jnp.einsum("hgqk,qhgd->khd", dscores, grouped, preferred_element_type=jnp.float32)
    dquery = unrotary(dquery, cosine, sine).reshape(length, D).astype(jnp.bfloat16)
    dkey = unrotary(dkey, cosine, sine).reshape(length, kv_width).astype(jnp.bfloat16)
    dqkv = jnp.concatenate([dquery, dkey, dvalues], axis=1)
    grad_qkv = left_product(normed_one, dqkv)
    grad_biases = jnp.sum(dqkv.astype(jnp.float32), axis=0)
    dnormed_one = narrowed(right_product(dqkv, full_qkv))
    dinput_norm, grad_gain_one = norm_back(dnormed_one, unit_one, factor_one, gain_one)
    input_grad = dmiddle + dinput_norm
    grad_attn = jnp.concatenate([grad_qkv, grad_out], axis=1)
    grad_lines = jnp.concatenate(
        [
            grad_gain_one.reshape(group, rows),
            grad_gain_two.reshape(group, rows),
            grad_biases.reshape(group, bias_rows),
        ],
        axis=1,
    )
    grad_lines = jnp.pad(grad_lines, ((0, 0), (0, attn_width - 2 * rows - bias_rows)))
    grad_attn = grad_attn.reshape(group, tall, attn_width)
    grad_attn = jnp.concatenate(
        [grad_attn[:, :rows], grad_lines[:, None], grad_attn[:, rows + 1 :]], axis=1
    ).reshape(group * tall, attn_width)
    part_down = group_total(grad_down)
    part_gate = group_total(grad_gate)
    part_up = group_total(grad_up)
    grad_attn = lax.optimization_barrier(
        (grad_attn.astype(jnp.bfloat16), part_down, part_gate, part_up)
    )[0]
    part_attn = group_total(grad_attn)
    sum_down = total(part_down, down_tall)
    sum_gate = total(part_gate, tall)
    sum_up = total(part_up, tall)
    sum_attn = total(part_attn, tall)
    mom_attn = attn_block(mom_query, mom_key, mom_value, mom_out, gain_mom, bias_mom)
    whole_down = gathered_rows(
        renew(lengthened(mom_down, down_tall), sum_down, replica, down_size), group, down_rows
    )
    whole_gate = renew(lengthened(mom_gate, tall), sum_gate, replica, size)
    whole_up = renew(lengthened(mom_up, tall), sum_up, replica, size)
    whole_attn = renew(mom_attn, sum_attn, replica, size)
    new_gate = own_rows(whole_gate, place, group, rows)
    new_up = own_rows(whole_up, place, group, rows)
    new_down = own_rows(whole_down, place, group, down_rows)
    new_attn = own_rows(whole_attn, place, group, rows)
    new_line = lax.dynamic_slice_in_dim(whole_attn, place * tall + rows, 1, axis=0)[0].astype(jnp.float32)
    new_query = new_attn[:, :D]
    new_key = new_attn[:, D : D + kv_width]
    new_value = new_attn[:, D + kv_width : D + 2 * kv_width]
    new_out = new_attn[:, D + 2 * kv_width :]
    token_total = length * group * replicas
    gain_mom_new = new_line[: 2 * rows].reshape(2, rows)
    gains_new = gains - vector_rate * gain_mom_new / math.sqrt(token_total)
    bias_mom_new = new_line[2 * rows : 2 * rows + bias_rows]
    biases_new = biases - vector_rate * bias_mom_new / math.sqrt(token_total)
    odd = replica % 2 == 1
    flat_attn = gathered_rows(whole_attn, group, rows)
    square_query = flat_attn[:, :D]
    square_out = flat_attn[:, D + 2 * kv_width :]

    def row_gram(whole):
        gram = right_product(whole, whole).reshape(group, tall, group, tall)
        return gram[:, :rows, :, :rows].reshape(D, D)

    def column_gram(whole):
        return left_product(whole, whole)

    gram = lax.switch(
        jnp.minimum(place, 3),
        [
            lambda: row_gram(whole_gate),
            lambda: row_gram(whole_up),
            lambda: column_gram(whole_down),
            lambda: column_gram(jnp.where(odd, square_out, square_query)),
        ],
    )
    factor = orthogonal_factor(gram).astype(jnp.bfloat16)
    factors = lax.all_gather(factor, "shard", axis=0, tiled=False)
    pairs = [(item, item ^ 1) for item in range(replicas)]
    other = lax.ppermute(factors[3], "rep", pairs)
    factor_query = jnp.where(odd, other, factors[3])
    factor_out = jnp.where(odd, factors[3], other)
    wide = math.sqrt(w_gate.shape[1] / D)

    def slab(item):
        block = lax.dynamic_slice_in_dim(factors[item], place * rows, rows, axis=0)
        return spread(block, group, tall)

    step_gate = wide * product(slab(0), whole_gate)
    step_up = wide * product(slab(1), whole_up)
    step_down = product(new_down.astype(jnp.bfloat16), factors[2])
    step_query = product(new_query.astype(jnp.bfloat16), factor_query)
    step_out = product(new_out.astype(jnp.bfloat16), factor_out)
    step_key = near(new_key, orthogonal_factor(column_gram(flat_attn[:, D : D + kv_width])))
    step_value = near(
        new_value, orthogonal_factor(column_gram(flat_attn[:, D + kv_width : D + 2 * kv_width]))
    )
    upd_gate = w_gate - muon_rate * step_gate
    upd_up = w_up - muon_rate * step_up
    upd_down = w_down - muon_rate * step_down
    upd_query = w_query - muon_rate * step_query
    upd_out = w_out - muon_rate * step_out
    upd_key = w_key - muon_rate * step_key
    upd_value = w_value - muon_rate * step_value
    return (
        result,
        input_grad,
        new_query,
        new_key,
        new_value,
        new_out,
        new_gate,
        new_up,
        new_down,
        upd_query,
        upd_key,
        upd_value,
        upd_out,
        upd_gate,
        upd_up,
        upd_down,
        gain_mom_new,
        gains_new,
        bias_mom_new,
        biases_new,
    )


def solution(mesh):
    placed = (
        P(("shard", "rep"), None),
        P(("shard", "rep"), None),
        P(("shard", "rep"), None),
        P("shard", None),
        P("shard", None),
        P("shard", None),
        P("shard", None),
        P("shard", None),
        P("shard", None),
        P("shard", None),
        P(None, "shard"),
        P("shard"),
        P("shard", None),
        P("shard", None),
        P("shard", None),
        P("shard", None),
        P("shard", None),
        P("shard", None),
        P("shard", None),
        P(None, "shard"),
        P("shard"),
    )
    return jax.shard_map(
        local,
        mesh=mesh,
        in_specs=placed,
        out_specs=(
            P(("shard", "rep"), None),
            P(("shard", "rep"), None),
            P("shard", None),
            P("shard", None),
            P("shard", None),
            P("shard", None),
            P("shard", None),
            P("shard", None),
            P("shard", None),
            P("shard", None),
            P("shard", None),
            P("shard", None),
            P("shard", None),
            P("shard", None),
            P("shard", None),
            P("shard", None),
            P(None, "shard"),
            P(None, "shard"),
            P("shard"),
            P("shard"),
        ),
        check_vma=False,
    )
```
